32 devices in a mesh: groups: 2 (over x), tm: 8 (over z, y), mp: 2 (over core).
Axes of the slice: x: 2, y: 2, z: 4, core: 2. Of those that a mesh axis runs over, the one named last changes fastest.
Arguments:
- branch_x: bfloat16 [8192, 4096], P(('groups', 'tm'), 'mp'), parts along dimension 0, may hold values from -6 to 6
- branch_y: bfloat16 [8192, 4096], P(('groups', 'tm'), 'mp'), parts along dimension 0, may hold values from -6 to 6
- queries: bfloat16 [8192, 4096], P(('groups', 'tm'), 'mp'), parts along dimension 0, may hold values from -1500 to 1500
- conv_weight: float32 [4, 4096], P(None, 'mp'), may hold values from -3 to 3
- conv_bias: float32 [4096], P('mp'), may hold values from -3 to 3
- gate_panel: bfloat16 [16, 256, 512], P('mp'), may hold values from -0.375 to 0.375
- gate_scale: float32 [16, 2, 512], P('mp'), may hold values from 0.5 to 2
- gate_bias: float32 [2, 4096], P(None, 'mp'), may hold values from -4 to 4
- decay_rate: float32 [4096], P('mp'), may hold values from 2.4414063e-05 to 0.05
- kv_panel: bfloat16 [4096, 512], P('mp'), may hold values from -0.09375 to 0.09375
- kv_scale: float32 [32, 512], P('mp'), may hold values from 0.5 to 2
- segment_ids: int32 [8192], P('groups'), parts along dimension 0, may hold values from 0 to 3, never falling along the last dimension, each value on 1 to 2048 neighbouring positions
Outputs:
- mixed: bfloat16 [8192, 4096], P(('groups', 'tm'), 'mp'), parts along dimension 0
- attended: bfloat16 [8192, 4096], P(('groups', 'tm'), 'mp'), parts along dimension 0
The draws below stay inside these ranges and needn't reach their ends.
There are 2 independent parts, one for each index of `groups`. The reference program is written for one: setup_inputs(seed, part) draws one part's arguments, and reference() takes and returns one part's arrays. A program takes and returns all parts, laid end to end along the dimension named above; an argument that names none is the same for every part. Nothing has to cross between parts.
Inputs may be any that keep to these rules, and one draw needn't show every extreme that they name: `segment_ids`: never falls along the sequence; each of the 4 documents holds 1 to 2048 positions, one of them exactly 2048.
All inputs are finite; a program needn't handle non-finite values.
Results may differ from the reference program's by a relative error of at most 0.03.
Values may be sent and summed in bfloat16 or wider, within the bound.
A program may use at most 128 MiB of HBM per device.

```python
import math
import jax
import jax.numpy as jnp
import numpy as np
from jax import lax

D = 4096
HEADS = 16
HD = 256
BLOCKS = 16
CONV = 4
WINDOW = 2048
SCALE_ROWS = 128
DOCS = 4
TOK_DEV = 512
SEQ = 4096
BW = 256


def draw_queries(key, part):
    normal_part = jnp.clip(jax.random.normal(key, (SEQ, HEADS * HD), jnp.float32), -6.0, 6.0)
    return normal_part.astype(jnp.bfloat16)


def draw_decay_rate(key, part):
    uniform_part = jax.random.uniform(key, (D,), jnp.float32)
    lowest = jnp.log(0.25 / SEQ)
    return jnp.exp(lowest + uniform_part * (jnp.log(0.05) - lowest))


def block_scale(key, shape, shards, least, largest):
    level, own = 1.0, jax.random.fold_in(key, 6)
    for axis_at, shards_of in shards:
        heights = jnp.exp(jax.random.uniform(jax.random.fold_in(own, axis_at), (shards_of,), jnp.float32, least / len(shards), largest / len(shards)))
        level = level * jnp.repeat(heights, shape[axis_at] // shards_of).reshape([-1 if axis == axis_at else 1 for axis in range(len(shape))])
    return level


def split_up(number_of, total, limit, lean):
    weights = [(1 << 20) // math.isqrt(rank ** lean) + 1 for rank in range(2, number_of + 1)]
    rest, given = total - limit - (number_of - 1), [1] * (number_of - 1)
    while rest > 0:
        movable = [i for i in range(number_of - 1) if given[i] < limit]
        mass, remaining = sum([weights[i] for i in movable]), rest
        for i in movable:
            more = min(limit - given[i], max(1, remaining * weights[i] // mass), rest)
            given[i] = given[i] + more
            rest = rest - more
    return np.array([limit] + given)


def ragged(stream_key, number_of, total, limit, lean):
    if number_of == 2:
        one = jax.random.randint(stream_key, (), max(1, total - limit), min(limit, total - 1) + 1)
        return jnp.stack([one, total - one])
    sizes = jnp.asarray(split_up(number_of, total, limit, lean), jnp.int32)
    twos = (number_of - 1) // 2
    donor, receiver = sizes[1:1 + 2 * twos:2], sizes[2:2 + 2 * twos:2]
    margin = jnp.minimum(donor - 1, limit - receiver)
    passed = jax.random.randint(jax.random.fold_in(stream_key, 1), (twos,), 0, 1 << 20) % (margin + 1)
    sizes = sizes.at[1:1 + 2 * twos:2].set(donor - passed).at[2:2 + 2 * twos:2].set(receiver + passed)
    return sizes[jax.random.permutation(jax.random.fold_in(stream_key, 2), number_of)]


def gaussian(stream_key, dims, scale, limit, cuts=(), kind=jnp.bfloat16):
    values = jax.random.normal(stream_key, dims, jnp.float32) * scale
    if len(cuts) > 0:
        values = block_scale(stream_key, dims, cuts, -0.22, 0.18) * values
    return jnp.clip(values, min=-limit, max=limit).astype(kind)


def setup_inputs(seed: int = 0, part: int = 0) -> dict:
    key_of = jax.random.split(jax.random.key(seed), 13)
    own_keys = jax.random.split(jax.random.fold_in(key_of[12], part), 13)
    branch_x = gaussian(own_keys[0], (SEQ, D), 1.0, 6.0, ((0, 8), (1, 2)))
    branch_y = gaussian(own_keys[1], (SEQ, D), 1.0, 6.0, ((0, 8), (1, 2)))
    queries = draw_queries(jax.random.fold_in(jax.random.fold_in(key_of[12], part), 71), part)
    conv_weight = gaussian(key_of[3], (CONV, D), 0.5, 3.0, ((1, 2),), jnp.float32)
    conv_bias = gaussian(key_of[4], (D,), 0.5, 3.0, ((0, 2),), jnp.float32)
    gate_panel = gaussian(key_of[5], (BLOCKS, BW, 2 * BW), BW ** -0.5, 0.375, ((0, 2),))
    gate_scale = jnp.clip(jnp.exp(math.log(2.0) - 1.3862944 * jax.random.uniform(key_of[6], (BLOCKS, BW // SCALE_ROWS, 2 * BW), jnp.float32) ** block_scale(key_of[6], (BLOCKS, BW // SCALE_ROWS, 2 * BW), ((0, 2),), -0.2, 0.2)), 0.5, 2.0)
    gate_bias = gaussian(key_of[7], (2, D), 1.0, 4.0, ((1, 2),), jnp.float32)
    decay_rate = draw_decay_rate(jax.random.fold_in(key_of[12], 71), part)
    kv_panel = gaussian(key_of[9], (D, 2 * HD), D ** -0.5, 0.09375, ((0, 2),))
    kv_scale = jnp.clip(jnp.exp(math.log(2.0) - 1.3862944 * jax.random.uniform(key_of[10], (D // SCALE_ROWS, 2 * HD), jnp.float32) ** block_scale(key_of[10], (D // SCALE_ROWS, 2 * HD), ((0, 2),), -0.2, 0.2)), 0.5, 2.0)
    segment_ids = jnp.searchsorted(jnp.cumsum(ragged(own_keys[11], DOCS, SEQ, SEQ // 2, 2)), jnp.arange(SEQ), side="right").astype(jnp.int32)
    return dict(branch_x=branch_x, branch_y=branch_y, queries=queries, conv_weight=conv_weight, conv_bias=conv_bias, gate_panel=gate_panel, gate_scale=gate_scale, gate_bias=gate_bias, decay_rate=decay_rate, kv_panel=kv_panel, kv_scale=kv_scale, segment_ids=segment_ids)


def dequantize(weight_panel, scales):
    row_count = weight_panel.shape[-2]
    shaped = weight_panel.astype(jnp.float32).reshape(weight_panel.shape[:-2] + (row_count // SCALE_ROWS, SCALE_ROWS, weight_panel.shape[-1]))
    return (shaped * jnp.expand_dims(scales, -2)).reshape(weight_panel.shape).astype(jnp.bfloat16)

def recur_step(state, inputs):
    nxt = inputs[0] * state + inputs[1]
    return (nxt, nxt)

def reference(branch_x, branch_y, queries, conv_weight, conv_bias, gate_panel, gate_scale, gate_bias, decay_rate, kv_panel, kv_scale, segment_ids):
    length = branch_x.shape[0]
    padded_ids = jnp.concatenate([-jnp.ones((WINDOW,), jnp.int32), segment_ids.astype(jnp.int32)])
    own_ids = segment_ids.astype(jnp.int32)
    resets = padded_ids[WINDOW:] != padded_ids[WINDOW - 1:WINDOW - 1 + length]
    padded_x = jnp.concatenate([jnp.zeros((CONV - 1, D), jnp.bfloat16), branch_x], 0)
    conv_sum = jnp.zeros((length, D), jnp.float32)
    for lag_index in range(CONV):
        same_doc = (padded_ids[WINDOW - lag_index:WINDOW - lag_index + length] == own_ids).astype(jnp.float32)
        offset = CONV - 1 - lag_index
        conv_sum = conv_sum + conv_weight[lag_index] * padded_x[offset:offset + length].astype(jnp.float32) * same_doc[:, None]
    conv_out = (conv_sum + conv_bias).astype(jnp.bfloat16)
    gate_weight = dequantize(gate_panel, gate_scale)
    gate_pre = jnp.einsum('tbi,bio->tbo', conv_out.reshape(length, BLOCKS, BW).astype(jnp.float32), gate_weight.astype(jnp.float32), precision=lax.Precision.HIGHEST)
    recur_gate = jax.nn.sigmoid(gate_pre[..., :BW].reshape(length, D) + gate_bias[0])
    input_gate = jax.nn.sigmoid(gate_pre[..., BW:].reshape(length, D) + gate_bias[1])
    log_decay = -8.0 * recur_gate * decay_rate
    decay = jnp.where(resets[:, None], jnp.float32(0.0), jnp.exp(log_decay))
    normalizer = jnp.where(resets[:, None], jnp.float32(1.0), jnp.sqrt(-jnp.expm1(2.0 * log_decay)))
    scaled_input = input_gate * conv_out.astype(jnp.float32) * normalizer
    final_state, state = lax.scan(recur_step, jnp.zeros((D,), jnp.float32), (decay, scaled_input))
    mixed = (state * jax.nn.gelu(branch_y.astype(jnp.float32), approximate=True)).astype(jnp.bfloat16)
    keys_values = jnp.dot(mixed, dequantize(kv_panel, kv_scale), preferred_element_type=jnp.float32).astype(jnp.bfloat16)
    padded_keys = jnp.concatenate([jnp.zeros((WINDOW, HD), jnp.bfloat16), keys_values[:, :HD]], 0)
    padded_values = jnp.concatenate([jnp.zeros((WINDOW, HD), jnp.bfloat16), keys_values[:, HD:]], 0)
    query_heads = queries.reshape(length, HEADS, HD)

    def one_block(block_index):
        first_row = block_index * TOK_DEV
        query_block = lax.dynamic_slice_in_dim(query_heads, first_row, TOK_DEV, 0)
        key_block = lax.dynamic_slice_in_dim(padded_keys, first_row, WINDOW + TOK_DEV, 0)
        value_block = lax.dynamic_slice_in_dim(padded_values, first_row, WINDOW + TOK_DEV, 0)
        key_ids = lax.dynamic_slice_in_dim(padded_ids, first_row, WINDOW + TOK_DEV)
        query_ids = lax.dynamic_slice_in_dim(own_ids, first_row, TOK_DEV)
        query_pos = first_row + jnp.arange(TOK_DEV, dtype=jnp.int32)
        key_pos = first_row - WINDOW + jnp.arange(WINDOW + TOK_DEV, dtype=jnp.int32)
        allowed = (key_pos[None, :] <= query_pos[:, None]) & (query_pos[:, None] - key_pos[None, :] < WINDOW) & (key_ids[None, :] == query_ids[:, None])
        scores = jnp.einsum('thd,sd->hts', query_block.astype(jnp.float32), key_block.astype(jnp.float32), precision=lax.Precision.HIGHEST) * HD ** (-0.5)
        scores = jnp.where(allowed[None], scores, jnp.float32(-1e+30))
        highest = lax.optimization_barrier(jnp.max(scores, axis=-1, keepdims=True))
        weights_raw = jnp.exp(scores - highest) * allowed[None].astype(jnp.float32)
        totals = lax.optimization_barrier(jnp.sum(weights_raw, axis=-1, keepdims=True))
        weights = (weights_raw / totals).astype(jnp.bfloat16)
        result = jnp.einsum('hts,sd->thd', weights.astype(jnp.float32), value_block.astype(jnp.float32), precision=lax.Precision.HIGHEST)
        return result.astype(jnp.bfloat16).reshape(TOK_DEV, HEADS * HD)
    blocks_out = lax.map(one_block, jnp.arange(length // TOK_DEV, dtype=jnp.int32))
    attended = blocks_out.reshape(length, HEADS * HD)
    return (mixed, attended)
```

```python
import functools

import jax
import jax.numpy as jnp
from jax import lax
from jax.experimental import pallas as pl
from jax.experimental.pallas import tpu as pltpu
from jax.sharding import PartitionSpec as P

HD = 256
CONV = 4
WINDOW = 2048
SCALE_ROWS = 128
RUNS = 8
TILE = 256
MESH = pl.DeviceIdType.MESH


def sigmoid(x):
    return 0.5 + 0.5 * jnp.tanh(0.5 * x)


def gelu(x):
    return 0.5 * x * (1.0 + jnp.tanh(0.7978845608028654 * (x + 0.044715 * (x * x * x))))


def expm1_small(x):
    p = 1.0 / 5040.0
    for c in (1.0 / 720.0, 1.0 / 120.0, 1.0 / 24.0, 1.0 / 6.0, 0.5, 1.0):
        p = p * x + c
    return p * x


def scaled(panel, scale_lo, scale_hi):
    lo = panel[:SCALE_ROWS].astype(jnp.float32) * scale_lo
    hi = panel[SCALE_ROWS:].astype(jnp.float32) * scale_hi
    return jnp.concatenate([lo, hi], 0).astype(jnp.bfloat16)


def recur_kernel(
    n, x_hbm, y_hbm, gp_hbm, kvp_hbm, cw_ref, cb_ref, gs_ref, gb_ref, rate_ref, kvs_ref, masks_ref,
    mixed_hbm, kv_hbm,
    xv, yv, gpv, kvpv, xs, g, convb, pbuf, sbuf, gel, perm, unperm, halo, summ, gath, inc8,
    kvacc, kvrecv, kvbuf, mixv,
    load_sem, halo_sem, st_send, st_recv, kvx_sem, fwd_send, fwd_recv, pt_send, pt_recv, out_sem,
):
    me = lax.axis_index("tm")
    half = lax.axis_index("mp")
    T, C = xv.shape
    nb = C // HD
    steps = T // RUNS

    loads = [
        pltpu.make_async_copy(s, d, load_sem.at[i])
        for i, (s, d) in enumerate(((x_hbm, xv), (gp_hbm, gpv), (y_hbm, yv), (kvp_hbm, kvpv)))
    ]
    for c in loads:
        c.start()

    barrier = pltpu.get_barrier_semaphore()
    for k in range(1, n):
        pl.semaphore_signal(
            barrier, inc=1, device_id={"tm": lax.rem(me + k, n)}, device_id_type=MESH
        )
    pl.semaphore_signal(barrier, inc=1, device_id={"mp": 1 - half}, device_id_type=MESH)

    row = lax.broadcasted_iota(jnp.int32, (T, T), 0)
    col = lax.broadcasted_iota(jnp.int32, (T, T), 1)
    sh = steps.bit_length() - 1
    at_row = lax.bitwise_and(row, RUNS - 1) * steps + lax.shift_right_logical(row, 3)
    perm[...] = (at_row == col).astype(jnp.float32).astype(jnp.bfloat16)
    at_col = lax.bitwise_and(col, RUNS - 1) * steps + lax.shift_right_logical(col, 3)
    unperm[...] = (at_col == row).astype(jnp.float32).astype(jnp.bfloat16)

    pl.semaphore_wait(barrier, n)
    halo_copy = pltpu.make_async_remote_copy(
        src_ref=x_hbm.at[pl.ds(T - 16, 16), :], dst_ref=halo,
        send_sem=halo_sem.at[0], recv_sem=halo_sem.at[1],
        device_id={"tm": lax.rem(me + 1, n)}, device_id_type=MESH,
    )

    @pl.when(me < n - 1)
    def _():
        halo_copy.start()

    @pl.when(me == 0)
    def _():
        halo[...] = jnp.zeros_like(halo)

    loads[0].wait()

    @pl.when(me > 0)
    def _():
        halo_copy.wait_recv()

    loads[1].wait()

    def block(b, _):
        cs = pl.ds(pl.multiple_of(b * HD, HD), HD)
        xp = jnp.dot(perm[...], xv[:, cs], preferred_element_type=jnp.float32)
        xs[pl.ds(24, T), :] = xp
        first = lax.broadcasted_iota(jnp.int32, (RUNS, HD), 0) == 0
        halo_f = halo[:, cs].astype(jnp.float32)
        for j in range(1, CONV):
            tail = xs[pl.ds(24 + T - 8 * j, 8), :]
            rolled = pltpu.roll(tail, 1, 0)
            xs[pl.ds(24 - 8 * j, 8), :] = jnp.where(first, halo_f[16 - j:17 - j], rolled)
        bias = cb_ref[:, cs]
        taps = [cw_ref[pl.ds(j, 1), cs] for j in range(CONV)]

        def conv_rows(i, _):
            r0 = pl.multiple_of(i * 64, 64)
            total = taps[0] * xs[pl.ds(r0 + 24, 64), :]
            for j in range(1, CONV):
                same = masks_ref[pl.ds(r0, 64), j - 1:j]
                total = total + taps[j] * (xs[pl.ds(r0 + 24 - 8 * j, 64), :] * same)
            convb[pl.ds(r0, 64), :] = (total + bias).astype(jnp.bfloat16)
            return 0

        lax.fori_loop(0, T // 64, conv_rows, 0)
        scales = gs_ref[b]
        gw = scaled(gpv[b], scales[0:1], scales[1:2])
        g[...] = jnp.dot(convb[...], gw, preferred_element_type=jnp.float32)
        b0, b1 = gb_ref[0:1, cs], gb_ref[1:2, cs]
        rate = -8.0 * rate_ref[:, cs]

        def rows(i, carry):
            prod, state = carry
            r0 = pl.multiple_of(i * 32, 32)
            rs = pl.ds(r0, 32)
            recur = sigmoid(g[rs, :HD] + b0)
            gate = sigmoid(g[rs, HD:] + b1)
            keep = masks_ref[rs, 0:1]
            e = expm1_small(recur * rate)
            a = (1.0 + e) * keep
            q = -e * (2.0 + e)
            m = q * lax.rsqrt(jnp.maximum(q, 1e-37))
            m = 1.0 + keep * (m - 1.0)
            u = gate * convb[rs, :].astype(jnp.float32) * m
            for k in range(4):
                ak = a[8 * k:8 * k + 8]
                prod = ak * prod
                state = ak * state + u[8 * k:8 * k + 8]
                pbuf[pl.ds(r0 + 8 * k, 8), cs] = prod
                sbuf[pl.ds(r0 + 8 * k, 8), cs] = state
            return prod, state

        lax.fori_loop(
            0, T // 32, rows, (jnp.ones((RUNS, HD), jnp.float32), jnp.zeros((RUNS, HD), jnp.float32))
        )
        return 0

    lax.fori_loop(0, nb, block, 0)

    p_end = pbuf[pl.ds(T - 8, 8), :]
    s_end = sbuf[pl.ds(T - 8, 8), :]
    dp, ds = p_end[0:1], s_end[0:1]
    for s in range(1, RUNS):
        ds = p_end[s:s + 1] * ds + s_end[s:s + 1]
        dp = p_end[s:s + 1] * dp
    summ[0:1, :] = dp
    summ[1:2, :] = ds

    def state_copy(k):
        return pltpu.make_async_remote_copy(
            src_ref=summ, dst_ref=gath.at[k], send_sem=st_send.at[k], recv_sem=st_recv.at[k],
            device_id={"tm": lax.rem(me + k, n)}, device_id_type=MESH,
        )

    for k in range(1, n):
        @pl.when(me + k < n)
        def _(k=k):
            state_copy(k).start()

    loads[2].wait()

    def gelu_block(b, _):
        cs = pl.ds(pl.multiple_of(b * HD, HD), HD)
        gel[:, cs] = gelu(jnp.dot(perm[...], yv[:, cs], preferred_element_type=jnp.float32))
        return 0

    lax.fori_loop(0, nb, gelu_block, 0)
    loads[3].wait()

    inc8[0:1, :] = jnp.zeros((1, C), jnp.float32)
    for k in range(n - 1, 0, -1):
        @pl.when(me >= k)
        def _(k=k):
            state_copy(k).wait_recv()
            inc8[0:1, :] = gath[k, 0:1, :] * inc8[0:1, :] + gath[k, 1:2, :]
    cur = inc8[0:1, :]
    for s in range(RUNS - 1):
        cur = p_end[s:s + 1] * cur + s_end[s:s + 1]
        inc8[s + 1:s + 2, :] = cur

    kvacc[...] = jnp.zeros_like(kvacc)

    def mix_block(b, _):
        cs = pl.ds(pl.multiple_of(b * HD, HD), HD)
        entering = jnp.concatenate([inc8[:, cs]] * 8, 0)

        def mix_rows(i, _):
            rs = pl.ds(pl.multiple_of(i * 64, 64), 64)
            state = sbuf[rs, cs] + pbuf[rs, cs] * entering
            convb[rs, :] = (state * gel[rs, cs]).astype(jnp.bfloat16)
            return 0

        lax.fori_loop(0, T // 64, mix_rows, 0)
        mixed = jnp.dot(
            unperm[...], convb[...], preferred_element_type=jnp.float32
        ).astype(jnp.bfloat16)
        mixv[:, cs] = mixed
        kw = scaled(
            kvpv[pl.ds(pl.multiple_of(b * HD, HD), HD), :],
            kvs_ref[pl.ds(2 * b, 1), :], kvs_ref[pl.ds(2 * b + 1, 1), :],
        )
        kvacc[...] += jnp.dot(mixed, kw, preferred_element_type=jnp.float32)
        return 0

    lax.fori_loop(0, nb, mix_block, 0)
    mixed_out = pltpu.make_async_copy(mixv, mixed_hbm, out_sem.at[0])
    mixed_out.start()

    own_cols = pl.ds(pl.multiple_of(half * HD, HD), HD)
    their_cols = pl.ds(pl.multiple_of((1 - half) * HD, HD), HD)
    partner = {"mp": 1 - half}
    exchange = pltpu.make_async_remote_copy(
        src_ref=kvacc.at[:, their_cols], dst_ref=kvrecv,
        send_sem=kvx_sem.at[0], recv_sem=kvx_sem.at[1], device_id=partner, device_id_type=MESH,
    )
    exchange.start()
    exchange.wait_recv()
    kvbuf[0, half] = (kvacc[:, own_cols] + kvrecv[...]).astype(jnp.bfloat16)

    odd = lax.rem(me, 2) == 1
    even = lax.rem(me, 2) == 0

    def forward(src, dst, sem, to):
        return pltpu.make_async_remote_copy(
            src_ref=kvbuf.at[src, half], dst_ref=kvbuf.at[dst, half],
            send_sem=fwd_send.at[sem], recv_sem=fwd_recv.at[dst],
            device_id={"tm": lax.rem(me + to + n, n)}, device_id_type=MESH,
        )

    def share(slot):
        return pltpu.make_async_remote_copy(
            src_ref=kvbuf.at[slot, half], dst_ref=kvbuf.at[slot, half],
            send_sem=pt_send.at[slot], recv_sem=pt_recv.at[slot],
            device_id=partner, device_id_type=MESH,
        )

    def arrived(slot):
        forward(0, slot, 0, 2).wait_recv()

    z_first, z_second = forward(0, 2, 0, 2), forward(2, 4, 1, 2)
    even_a, even_b = forward(0, 1, 2, 1), forward(2, 3, 3, 1)
    odd_a, odd_b = forward(2, 1, 2, -1), forward(4, 3, 3, -1)
    ahead = me + 2 < n

    def when(cond, do):
        pl.when(cond)(do)

    when(ahead, z_first.start)
    when(even, even_a.start)
    share(0).start()

    @pl.when(me >= 2)
    def _():
        arrived(2)
        when(ahead, z_second.start)
        when(even, even_b.start)
        when(odd, odd_a.start)
        share(2).start()

    @pl.when(me >= 1)
    def _():
        arrived(1)
        share(1).start()

    @pl.when(me >= 4)
    def _():
        arrived(4)
        when(odd, odd_b.start)
        share(4).start()

    @pl.when(me >= 3)
    def _():
        arrived(3)
        share(3).start()

    outs = [pltpu.make_async_copy(kvbuf.at[k], kv_hbm.at[4 - k], out_sem.at[1 + k]) for k in range(5)]
    for k in range(5):
        @pl.when(me >= k)
        def _(k=k):
            share(k).wait()
            outs[k].start()

    for k in range(1, n):
        @pl.when(me + k < n)
        def _(k=k):
            state_copy(k).wait_send()

    @pl.when(me < n - 1)
    def _():
        halo_copy.wait_send()

    exchange.wait_send()
    when(ahead, z_first.wait_send)
    when(even, even_a.wait_send)

    @pl.when(me >= 2)
    def _():
        when(ahead, z_second.wait_send)
        when(even, even_b.wait_send)
        when(odd, odd_a.wait_send)

    when(odd & (me >= 4), odd_b.wait_send)
    for k in range(5):
        when(me >= k, outs[k].wait)
    mixed_out.wait()


def attend_kernel(lo_ref, q_ref, kv_ref, qid_ref, kid_ref, mixed_in, o_ref, mixed_out, bias, scores, acc, top, low, sem):
    j = pl.program_id(0)
    heads = q_ref.shape[1] // HD
    pass_on = pltpu.make_async_copy(mixed_in, mixed_out, sem)

    @pl.when(j == 0)
    def _():
        pass_on.start()

    lo = lo_ref[j]
    hi = WINDOW // TILE + j + 1
    per = kv_ref.shape[2] // TILE
    c = HD ** (-0.5) * 1.4426950408889634
    qid = qid_ref[...]
    offset = lax.broadcasted_iota(jnp.int32, (TILE, TILE), 0) - lax.broadcasted_iota(
        jnp.int32, (TILE, TILE), 1
    )
    top[...] = jnp.full_like(top, -3e38)
    low[...] = jnp.zeros_like(low)
    acc[...] = jnp.zeros_like(acc)

    def score(t, _):
        blk, r = t // per, lax.rem(t, per)
        keys = kv_ref[blk, 0, pl.ds(pl.multiple_of(r * TILE, TILE), TILE), :]
        back = offset + (WINDOW + (j - t) * TILE)
        ok = (back >= 0) & (back < WINDOW) & (kid_ref[t] == qid)
        bias[...] = jnp.where(ok, 0.0, -1e30)
        for h in range(heads):
            s = lax.dot_general(
                q_ref[:, h * HD:(h + 1) * HD], keys, (((1,), (1,)), ((), ())),
                preferred_element_type=jnp.float32,
            ) + bias[...]
            scores[h, t] = s
            top[h] = jnp.maximum(top[h], jnp.maximum(s[:, :128], s[:, 128:]))
        return 0

    lax.fori_loop(lo, hi, score, 0)
    for h in range(heads):
        top[h] = jnp.broadcast_to(jnp.max(top[h], axis=1, keepdims=True), (TILE, 128))

    def weigh(t, _):
        blk, r = t // per, lax.rem(t, per)
        values = kv_ref[blk, 1, pl.ds(pl.multiple_of(r * TILE, TILE), TILE), :]
        for h in range(heads):
            m = top[h]
            s = scores[h, t]
            w = [jnp.exp2((s[:, i * 128:(i + 1) * 128] - m) * c) for i in range(2)]
            low[h] += w[0] + w[1]
            acc[h] += jnp.dot(
                jnp.concatenate(w, 1).astype(jnp.bfloat16), values, preferred_element_type=jnp.float32
            )
        return 0

    lax.fori_loop(lo, hi, weigh, 0)
    for h in range(heads):
        total = jnp.sum(low[h], axis=1, keepdims=True)
        o_ref[:, h * HD:(h + 1) * HD] = (acc[h] * (1.0 / total)).astype(jnp.bfloat16)

    @pl.when(j == pl.num_programs(0) - 1)
    def _():
        pass_on.wait()


def local(
    n, branch_x, branch_y, queries, conv_weight, conv_bias, gate_panel, gate_scale, gate_bias,
    decay_rate, kv_panel, kv_scale, segment_ids,
):
    T, C = branch_x.shape
    f32, bf16 = jnp.float32, jnp.bfloat16
    heads = queries.shape[1] // HD
    first_row = lax.axis_index("tm") * T
    padded_ids = jnp.concatenate([-jnp.ones((WINDOW,), jnp.int32), segment_ids])
    key_ids = lax.dynamic_slice_in_dim(padded_ids, first_row, WINDOW + T)
    own_ids = key_ids[WINDOW:]
    masks = jnp.stack(
        [(key_ids[WINDOW - j:WINDOW - j + T] == own_ids).astype(f32) for j in range(1, CONV)], -1
    )
    masks = masks.reshape(RUNS, T // RUNS, CONV - 1).transpose(1, 0, 2).reshape(T, CONV - 1)
    vmem, anyw = pl.BlockSpec(memory_space=pltpu.VMEM), pl.BlockSpec(memory_space=pl.ANY)
    dma = pltpu.SemaphoreType.DMA
    mixed, kv = pl.pallas_call(
        functools.partial(recur_kernel, n),
        out_shape=(
            jax.ShapeDtypeStruct((T, C), bf16), jax.ShapeDtypeStruct((5, 2, T, HD), bf16),
        ),
        in_specs=[anyw] * 4 + [vmem] * 7,
        out_specs=(anyw, anyw),
        scratch_shapes=[
            pltpu.VMEM((T, C), bf16), pltpu.VMEM((T, C), bf16),
            pltpu.VMEM(gate_panel.shape, bf16), pltpu.VMEM(kv_panel.shape, bf16),
            pltpu.VMEM((T + 24, HD), f32), pltpu.VMEM((T, 2 * HD), f32), pltpu.VMEM((T, HD), bf16),
            pltpu.VMEM((T, C), f32), pltpu.VMEM((T, C), f32), pltpu.VMEM((T, C), f32),
            pltpu.VMEM((T, T), bf16), pltpu.VMEM((T, T), bf16), pltpu.VMEM((16, C), bf16),
            pltpu.VMEM((2, C), f32), pltpu.VMEM((n, 2, C), f32), pltpu.VMEM((RUNS, C), f32),
            pltpu.VMEM((T, 2 * HD), f32), pltpu.VMEM((T, HD), f32),
            pltpu.VMEM((5, 2, T, HD), bf16), pltpu.VMEM((T, C), bf16),
            dma((4,)), dma((2,)), dma((n,)), dma((n,)), dma((2,)), dma((4,)), dma((5,)),
            dma((5,)), dma((5,)), dma((6,)),
        ],
        compiler_params=pltpu.CompilerParams(
            collective_id=0, has_side_effects=True, vmem_limit_bytes=56 * 1024 * 1024
        ),
        name="recurrence",
    )(
        branch_x, branch_y, gate_panel, kv_panel, conv_weight, conv_bias[None], gate_scale,
        gate_bias, decay_rate[None], kv_scale, masks,
    )
    tiles = (WINDOW + T) // TILE
    row0 = jnp.arange(T // TILE, dtype=jnp.int32) * TILE
    doc = jnp.sum((key_ids[None, :] < own_ids[::TILE][:, None]).astype(jnp.int32), 1)
    lo = jnp.maximum(doc, row0 + 1) // TILE
    attended, mixed = pl.pallas_call(
        attend_kernel,
        out_shape=(
            jax.ShapeDtypeStruct(queries.shape, bf16), jax.ShapeDtypeStruct((T, C), bf16),
        ),
        grid_spec=pltpu.PrefetchScalarGridSpec(
            num_scalar_prefetch=1,
            grid=(T // TILE,),
            in_specs=[
                pl.BlockSpec((TILE, heads * HD), lambda j, lo: (j, 0)),
                pl.BlockSpec(memory_space=pltpu.VMEM),
                pl.BlockSpec((TILE, 1), lambda j, lo: (j, 0)),
                pl.BlockSpec(memory_space=pltpu.VMEM),
                anyw,
            ],
            out_specs=(pl.BlockSpec((TILE, heads * HD), lambda j, lo: (j, 0)), anyw),
            scratch_shapes=[
                pltpu.VMEM((TILE, TILE), f32), pltpu.VMEM((heads, tiles, TILE, TILE), f32),
                pltpu.VMEM((heads, TILE, HD), f32), pltpu.VMEM((heads, TILE, 128), f32),
                pltpu.VMEM((heads, TILE, 128), f32), dma,
            ],
        ),
        compiler_params=pltpu.CompilerParams(vmem_limit_bytes=56 * 1024 * 1024),
        name="attention",
    )(lo, queries, kv, own_ids[:, None], key_ids.reshape(tiles, 1, TILE), mixed)
    return (mixed, attended)


def solution(mesh):
    rows = P(("groups", "tm"), "mp")
    in_specs = (
        rows, rows, rows, P(None, "mp"), P("mp"), P("mp", None, None), P("mp", None, None),
        P(None, "mp"), P("mp"), P("mp", None), P("mp", None), P("groups"),
    )
    return jax.shard_map(
        functools.partial(local, mesh.shape["tm"]), mesh=mesh, in_specs=in_specs,
        out_specs=(rows, rows), check_vma=False,
    )
```

```python
import functools

import jax
import jax.numpy as jnp
from jax import lax
from jax.experimental import pallas as pl
from jax.experimental.pallas import tpu as pltpu
from jax.sharding import PartitionSpec as P

HD = 256
CONV = 4
WINDOW = 2048
SCALE_ROWS = 128
RUNS = 8
TILE = 256
MESH = pl.DeviceIdType.MESH


def sigmoid(x):
    return 0.5 + 0.5 * jnp.tanh(0.5 * x)


def gelu(x):
    return 0.5 * x * (1.0 + jnp.tanh(0.7978845608028654 * (x + 0.044715 * (x * x * x))))


def expm1_small(x):
    p = 1.0 / 5040.0
    for c in (1.0 / 720.0, 1.0 / 120.0, 1.0 / 24.0, 1.0 / 6.0, 0.5, 1.0):
        p = p * x + c
    return p * x


def scaled(panel, scale_lo, scale_hi):
    lo = panel[:SCALE_ROWS].astype(jnp.float32) * scale_lo
    hi = panel[SCALE_ROWS:].astype(jnp.float32) * scale_hi
    return jnp.concatenate([lo, hi], 0).astype(jnp.bfloat16)


def recur_kernel(
    n, x_hbm, y_hbm, gp_hbm, kvp_hbm, cw_ref, cb_ref, gs_ref, gb_ref, rate_ref, kvs_ref, masks_ref,
    mixed_hbm, kv_hbm,
    xv, yv, gpv, kvpv, xs, g, convb, pbuf, sbuf, gel, perm, unperm, halo, summ, gath, inc8,
    kvacc, kvrecv, kvbuf, mixv,
    load_sem, halo_sem, st_send, st_recv, kvx_sem, fwd_send, fwd_recv, pt_send, pt_recv, out_sem,
):
    me = lax.axis_index("tm")
    half = lax.axis_index("mp")
    T, C = xv.shape
    nb = C // HD
    steps = T // RUNS

    loads = [
        pltpu.make_async_copy(s, d, load_sem.at[i])
        for i, (s, d) in enumerate(((x_hbm, xv), (gp_hbm, gpv), (y_hbm, yv), (kvp_hbm, kvpv)))
    ]
    for c in loads:
        c.start()

    barrier = pltpu.get_barrier_semaphore()
    for k in range(1, n):
        pl.semaphore_signal(
            barrier, inc=1, device_id={"tm": lax.rem(me + k, n)}, device_id_type=MESH
        )
    pl.semaphore_signal(barrier, inc=1, device_id={"mp": 1 - half}, device_id_type=MESH)

    row = lax.broadcasted_iota(jnp.int32, (T, T), 0)
    col = lax.broadcasted_iota(jnp.int32, (T, T), 1)
    sh = steps.bit_length() - 1
    at_row = lax.bitwise_and(row, RUNS - 1) * steps + lax.shift_right_logical(row, 3)
    perm[...] = (at_row == col).astype(jnp.float32).astype(jnp.bfloat16)
    at_col = lax.bitwise_and(col, RUNS - 1) * steps + lax.shift_right_logical(col, 3)
    unperm[...] = (at_col == row).astype(jnp.float32).astype(jnp.bfloat16)

    pl.semaphore_wait(barrier, n)
    halo_copy = pltpu.make_async_remote_copy(
        src_ref=x_hbm.at[pl.ds(T - 16, 16), :], dst_ref=halo,
        send_sem=halo_sem.at[0], recv_sem=halo_sem.at[1],
        device_id={"tm": lax.rem(me + 1, n)}, device_id_type=MESH,
    )

    @pl.when(me < n - 1)
    def _():
        halo_copy.start()

    @pl.when(me == 0)
    def _():
        halo[...] = jnp.zeros_like(halo)

    loads[0].wait()

    @pl.when(me > 0)
    def _():
        halo_copy.wait_recv()

    loads[1].wait()

    def block(b, _):
        cs = pl.ds(pl.multiple_of(b * HD, HD), HD)
        xp = jnp.dot(perm[...], xv[:, cs], preferred_element_type=jnp.float32)
        xs[pl.ds(24, T), :] = xp
        first = lax.broadcasted_iota(jnp.int32, (RUNS, HD), 0) == 0
        halo_f = halo[:, cs].astype(jnp.float32)
        for j in range(1, CONV):
            tail = xs[pl.ds(24 + T - 8 * j, 8), :]
            rolled = pltpu.roll(tail, 1, 0)
            xs[pl.ds(24 - 8 * j, 8), :] = jnp.where(first, halo_f[16 - j:17 - j], rolled)
        bias = cb_ref[:, cs]
        taps = [cw_ref[pl.ds(j, 1), cs] for j in range(CONV)]

        def conv_rows(i, _):
            r0 = pl.multiple_of(i * 64, 64)
            total = taps[0] * xs[pl.ds(r0 + 24, 64), :]
            for j in range(1, CONV):
                same = masks_ref[pl.ds(r0, 64), j - 1:j]
                total = total + taps[j] * (xs[pl.ds(r0 + 24 - 8 * j, 64), :] * same)
            convb[pl.ds(r0, 64), :] = (total + bias).astype(jnp.bfloat16)
            return 0

        lax.fori_loop(0, T // 64, conv_rows, 0)
        scales = gs_ref[b]
        gw = scaled(gpv[b], scales[0:1], scales[1:2])
        g[...] = jnp.dot(convb[...], gw, preferred_element_type=jnp.float32)
        b0, b1 = gb_ref[0:1, cs], gb_ref[1:2, cs]
        rate = -8.0 * rate_ref[:, cs]

        def rows(i, carry):
            prod, state = carry
            r0 = pl.multiple_of(i * 64, 64)
            rs = pl.ds(r0, 64)
            recur = sigmoid(g[rs, :HD] + b0)
            gate = sigmoid(g[rs, HD:] + b1)
            keep = masks_ref[rs, 0:1]
            e = expm1_small(recur * rate)
            a = (1.0 + e) * keep
            q = -e * (2.0 + e)
            m = q * lax.rsqrt(jnp.maximum(q, 1e-37))
            m = 1.0 + keep * (m - 1.0)
            u = gate * convb[rs, :].astype(jnp.float32) * m
            for k in range(8):
                ak = a[8 * k:8 * k + 8]
                prod = ak * prod
                state = ak * state + u[8 * k:8 * k + 8]
                pbuf[pl.ds(r0 + 8 * k, 8), cs] = prod
                sbuf[pl.ds(r0 + 8 * k, 8), cs] = state
            return prod, state

        lax.fori_loop(
            0, T // 64, rows, (jnp.ones((RUNS, HD), jnp.float32), jnp.zeros((RUNS, HD), jnp.float32))
        )
        return 0

    lax.fori_loop(0, nb, block, 0)

    p_end = pbuf[pl.ds(T - 8, 8), :]
    s_end = sbuf[pl.ds(T - 8, 8), :]
    dp, ds = p_end[0:1], s_end[0:1]
    for s in range(1, RUNS):
        ds = p_end[s:s + 1] * ds + s_end[s:s + 1]
        dp = p_end[s:s + 1] * dp
    summ[0:1, :] = dp
    summ[1:2, :] = ds

    def state_copy(k):
        return pltpu.make_async_remote_copy(
            src_ref=summ, dst_ref=gath.at[k], send_sem=st_send.at[k], recv_sem=st_recv.at[k],
            device_id={"tm": lax.rem(me + k, n)}, device_id_type=MESH,
        )

    for k in range(1, n):
        @pl.when(me + k < n)
        def _(k=k):
            state_copy(k).start()

    loads[2].wait()

    def gelu_block(b, _):
        cs = pl.ds(pl.multiple_of(b * HD, HD), HD)
        gel[:, cs] = gelu(jnp.dot(perm[...], yv[:, cs], preferred_element_type=jnp.float32))
        return 0

    lax.fori_loop(0, nb, gelu_block, 0)
    loads[3].wait()

    inc8[0:1, :] = jnp.zeros((1, C), jnp.float32)
    for k in range(n - 1, 0, -1):
        @pl.when(me >= k)
        def _(k=k):
            state_copy(k).wait_recv()
            inc8[0:1, :] = gath[k, 0:1, :] * inc8[0:1, :] + gath[k, 1:2, :]
    cur = inc8[0:1, :]
    for s in range(RUNS - 1):
        cur = p_end[s:s + 1] * cur + s_end[s:s + 1]
        inc8[s + 1:s + 2, :] = cur

    kvacc[...] = jnp.zeros_like(kvacc)

    def mix_block(b, _):
        cs = pl.ds(pl.multiple_of(b * HD, HD), HD)
        entering = jnp.concatenate([inc8[:, cs]] * 8, 0)

        def mix_rows(i, _):
            rs = pl.ds(pl.multiple_of(i * 64, 64), 64)
            state = sbuf[rs, cs] + pbuf[rs, cs] * entering
            convb[rs, :] = (state * gel[rs, cs]).astype(jnp.bfloat16)
            return 0

        lax.fori_loop(0, T // 64, mix_rows, 0)
        mixed = jnp.dot(
            unperm[...], convb[...], preferred_element_type=jnp.float32
        ).astype(jnp.bfloat16)
        mixv[:, cs] = mixed
        kw = scaled(
            kvpv[pl.ds(pl.multiple_of(b * HD, HD), HD), :],
            kvs_ref[pl.ds(2 * b, 1), :], kvs_ref[pl.ds(2 * b + 1, 1), :],
        )
        kvacc[...] += jnp.dot(mixed, kw, preferred_element_type=jnp.float32)
        return 0

    lax.fori_loop(0, nb, mix_block, 0)
    mixed_out = pltpu.make_async_copy(mixv, mixed_hbm, out_sem.at[0])
    mixed_out.start()

    own_cols = pl.ds(pl.multiple_of(half * HD, HD), HD)
    their_cols = pl.ds(pl.multiple_of((1 - half) * HD, HD), HD)
    partner = {"mp": 1 - half}
    exchange = pltpu.make_async_remote_copy(
        src_ref=kvacc.at[:, their_cols], dst_ref=kvrecv,
        send_sem=kvx_sem.at[0], recv_sem=kvx_sem.at[1], device_id=partner, device_id_type=MESH,
    )
    exchange.start()
    exchange.wait_recv()
    kvbuf[0, half] = (kvacc[:, own_cols] + kvrecv[...]).astype(jnp.bfloat16)

    odd = lax.rem(me, 2) == 1
    even = lax.rem(me, 2) == 0

    def forward(src, dst, sem, to):
        return pltpu.make_async_remote_copy(
            src_ref=kvbuf.at[src, half], dst_ref=kvbuf.at[dst, half],
            send_sem=fwd_send.at[sem], recv_sem=fwd_recv.at[dst],
            device_id={"tm": lax.rem(me + to + n, n)}, device_id_type=MESH,
        )

    def share(slot):
        return pltpu.make_async_remote_copy(
            src_ref=kvbuf.at[slot, half], dst_ref=kvbuf.at[slot, half],
            send_sem=pt_send.at[slot], recv_sem=pt_recv.at[slot],
            device_id=partner, device_id_type=MESH,
        )

    def arrived(slot):
        forward(0, slot, 0, 2).wait_recv()

    z_first, z_second = forward(0, 2, 0, 2), forward(2, 4, 1, 2)
    even_a, even_b = forward(0, 1, 2, 1), forward(2, 3, 3, 1)
    odd_a, odd_b = forward(2, 1, 2, -1), forward(4, 3, 3, -1)
    ahead = me + 2 < n

    def when(cond, do):
        pl.when(cond)(do)

    when(ahead, z_first.start)
    when(even, even_a.start)
    share(0).start()

    @pl.when(me >= 2)
    def _():
        arrived(2)
        when(ahead, z_second.start)
        when(even, even_b.start)
        when(odd, odd_a.start)
        share(2).start()

    @pl.when(me >= 1)
    def _():
        arrived(1)
        share(1).start()

    @pl.when(me >= 4)
    def _():
        arrived(4)
        when(odd, odd_b.start)
        share(4).start()

    @pl.when(me >= 3)
    def _():
        arrived(3)
        share(3).start()

    outs = [pltpu.make_async_copy(kvbuf.at[k], kv_hbm.at[4 - k], out_sem.at[1 + k]) for k in range(5)]
    for k in range(5):
        @pl.when(me >= k)
        def _(k=k):
            share(k).wait()
            outs[k].start()

    for k in range(1, n):
        @pl.when(me + k < n)
        def _(k=k):
            state_copy(k).wait_send()

    @pl.when(me < n - 1)
    def _():
        halo_copy.wait_send()

    exchange.wait_send()
    when(ahead, z_first.wait_send)
    when(even, even_a.wait_send)

    @pl.when(me >= 2)
    def _():
        when(ahead, z_second.wait_send)
        when(even, even_b.wait_send)
        when(odd, odd_a.wait_send)

    when(odd & (me >= 4), odd_b.wait_send)
    for k in range(5):
        when(me >= k, outs[k].wait)
    mixed_out.wait()


def attend_kernel(lo_ref, q_ref, kv_ref, qid_ref, kid_ref, mixed_in, o_ref, mixed_out, bias, scores, acc, top, low):
    j = pl.program_id(0)
    heads = q_ref.shape[1] // HD
    mixed_out[...] = mixed_in[...]
    lo = lo_ref[j]
    hi = WINDOW // TILE + j + 1
    per = kv_ref.shape[2] // TILE
    c = HD ** (-0.5) * 1.4426950408889634
    qid = qid_ref[...]
    offset = lax.broadcasted_iota(jnp.int32, (TILE, TILE), 0) - lax.broadcasted_iota(
        jnp.int32, (TILE, TILE), 1
    )
    top[...] = jnp.full_like(top, -3e38)
    low[...] = jnp.zeros_like(low)
    acc[...] = jnp.zeros_like(acc)

    def score(t, _):
        blk, r = t // per, lax.rem(t, per)
        keys = kv_ref[blk, 0, pl.ds(pl.multiple_of(r * TILE, TILE), TILE), :]
        back = offset + (WINDOW + (j - t) * TILE)
        ok = (back >= 0) & (back < WINDOW) & (kid_ref[t] == qid)
        bias[...] = jnp.where(ok, 0.0, -1e30)
        for h in range(heads):
            s = lax.dot_general(
                q_ref[:, h * HD:(h + 1) * HD], keys, (((1,), (1,)), ((), ())),
                preferred_element_type=jnp.float32,
            ) + bias[...]
            scores[h, t] = s
            top[h] = jnp.maximum(top[h], jnp.maximum(s[:, :128], s[:, 128:]))
        return 0

    lax.fori_loop(lo, hi, score, 0)
    for h in range(heads):
        top[h] = jnp.broadcast_to(jnp.max(top[h], axis=1, keepdims=True), (TILE, 128))

    def weigh(t, _):
        blk, r = t // per, lax.rem(t, per)
        values = kv_ref[blk, 1, pl.ds(pl.multiple_of(r * TILE, TILE), TILE), :]
        for h in range(heads):
            m = top[h]
            s = scores[h, t]
            w = [jnp.exp2((s[:, i * 128:(i + 1) * 128] - m) * c) for i in range(2)]
            low[h] += w[0] + w[1]
            acc[h] += jnp.dot(
                jnp.concatenate(w, 1).astype(jnp.bfloat16), values, preferred_element_type=jnp.float32
            )
        return 0

    lax.fori_loop(lo, hi, weigh, 0)
    for h in range(heads):
        total = jnp.sum(low[h], axis=1, keepdims=True)
        o_ref[:, h * HD:(h + 1) * HD] = (acc[h] * (1.0 / total)).astype(jnp.bfloat16)


def local(
    n, branch_x, branch_y, queries, conv_weight, conv_bias, gate_panel, gate_scale, gate_bias,
    decay_rate, kv_panel, kv_scale, segment_ids,
):
    T, C = branch_x.shape
    f32, bf16 = jnp.float32, jnp.bfloat16
    heads = queries.shape[1] // HD
    first_row = lax.axis_index("tm") * T
    padded_ids = jnp.concatenate([-jnp.ones((WINDOW,), jnp.int32), segment_ids])
    key_ids = lax.dynamic_slice_in_dim(padded_ids, first_row, WINDOW + T)
    own_ids = key_ids[WINDOW:]
    masks = jnp.stack(
        [(key_ids[WINDOW - j:WINDOW - j + T] == own_ids).astype(f32) for j in range(1, CONV)], -1
    )
    masks = masks.reshape(RUNS, T // RUNS, CONV - 1).transpose(1, 0, 2).reshape(T, CONV - 1)
    vmem, anyw = pl.BlockSpec(memory_space=pltpu.VMEM), pl.BlockSpec(memory_space=pl.ANY)
    dma = pltpu.SemaphoreType.DMA
    mixed, kv = pl.pallas_call(
        functools.partial(recur_kernel, n),
        out_shape=(
            jax.ShapeDtypeStruct((T, C), bf16), jax.ShapeDtypeStruct((5, 2, T, HD), bf16),
        ),
        in_specs=[anyw] * 4 + [vmem] * 7,
        out_specs=(anyw, anyw),
        scratch_shapes=[
            pltpu.VMEM((T, C), bf16), pltpu.VMEM((T, C), bf16),
            pltpu.VMEM(gate_panel.shape, bf16), pltpu.VMEM(kv_panel.shape, bf16),
            pltpu.VMEM((T + 24, HD), f32), pltpu.VMEM((T, 2 * HD), f32), pltpu.VMEM((T, HD), bf16),
            pltpu.VMEM((T, C), f32), pltpu.VMEM((T, C), f32), pltpu.VMEM((T, C), f32),
            pltpu.VMEM((T, T), bf16), pltpu.VMEM((T, T), bf16), pltpu.VMEM((16, C), bf16),
            pltpu.VMEM((2, C), f32), pltpu.VMEM((n, 2, C), f32), pltpu.VMEM((RUNS, C), f32),
            pltpu.VMEM((T, 2 * HD), f32), pltpu.VMEM((T, HD), f32),
            pltpu.VMEM((5, 2, T, HD), bf16), pltpu.VMEM((T, C), bf16),
            dma((4,)), dma((2,)), dma((n,)), dma((n,)), dma((2,)), dma((4,)), dma((5,)),
            dma((5,)), dma((5,)), dma((6,)),
        ],
        compiler_params=pltpu.CompilerParams(
            collective_id=0, has_side_effects=True, vmem_limit_bytes=56 * 1024 * 1024
        ),
        name="recurrence",
    )(
        branch_x, branch_y, gate_panel, kv_panel, conv_weight, conv_bias[None], gate_scale,
        gate_bias, decay_rate[None], kv_scale, masks,
    )
    tiles = (WINDOW + T) // TILE
    row0 = jnp.arange(T // TILE, dtype=jnp.int32) * TILE
    doc = jnp.sum((key_ids[None, :] < own_ids[::TILE][:, None]).astype(jnp.int32), 1)
    lo = jnp.maximum(doc, row0 + 1) // TILE
    attended, mixed = pl.pallas_call(
        attend_kernel,
        out_shape=(
            jax.ShapeDtypeStruct(queries.shape, bf16), jax.ShapeDtypeStruct((T, C), bf16),
        ),
        grid_spec=pltpu.PrefetchScalarGridSpec(
            num_scalar_prefetch=1,
            grid=(T // TILE,),
            in_specs=[
                pl.BlockSpec((TILE, heads * HD), lambda j, lo: (j, 0)),
                pl.BlockSpec(memory_space=pltpu.VMEM),
                pl.BlockSpec((TILE, 1), lambda j, lo: (j, 0)),
                pl.BlockSpec(memory_space=pltpu.VMEM),
                pl.BlockSpec((TILE, C), lambda j, lo: (j, 0)),
            ],
            out_specs=(
                pl.BlockSpec((TILE, heads * HD), lambda j, lo: (j, 0)),
                pl.BlockSpec((TILE, C), lambda j, lo: (j, 0)),
            ),
            scratch_shapes=[
                pltpu.VMEM((TILE, TILE), f32), pltpu.VMEM((heads, tiles, TILE, TILE), f32),
                pltpu.VMEM((heads, TILE, HD), f32), pltpu.VMEM((heads, TILE, 128), f32),
                pltpu.VMEM((heads, TILE, 128), f32),
            ],
        ),
        compiler_params=pltpu.CompilerParams(vmem_limit_bytes=56 * 1024 * 1024),
        name="attention",
    )(lo, queries, kv, own_ids[:, None], key_ids.reshape(tiles, 1, TILE), mixed)
    return (mixed, attended)


def solution(mesh):
    rows = P(("groups", "tm"), "mp")
    in_specs = (
        rows, rows, rows, P(None, "mp"), P("mp"), P("mp", None, None), P("mp", None, None),
        P(None, "mp"), P("mp"), P("mp", None), P("mp", None), P("groups"),
    )
    return jax.shard_map(
        functools.partial(local, mesh.shape["tm"]), mesh=mesh, in_specs=in_specs,
        out_specs=(rows, rows), check_vma=False,
    )
```

```python
import functools

import jax
import jax.numpy as jnp
from jax import lax
from jax.experimental import pallas as pl
from jax.experimental.pallas import tpu as pltpu
from jax.sharding import PartitionSpec as P

HD = 256
CONV = 4
WINDOW = 2048
SCALE_ROWS = 128
RUNS = 8
TILE = 256
MESH = pl.DeviceIdType.MESH


def sigmoid(x):
    return 0.5 + 0.5 * jnp.tanh(0.5 * x)


def gelu(x):
    return 0.5 * x * (1.0 + jnp.tanh(0.7978845608028654 * (x + 0.044715 * (x * x * x))))


def expm1_small(x):
    p = 1.0 / 5040.0
    for c in (1.0 / 720.0, 1.0 / 120.0, 1.0 / 24.0, 1.0 / 6.0, 0.5, 1.0):
        p = p * x + c
    return p * x


def scaled(panel, scale_lo, scale_hi):
    lo = panel[:SCALE_ROWS].astype(jnp.float32) * scale_lo
    hi = panel[SCALE_ROWS:].astype(jnp.float32) * scale_hi
    return jnp.concatenate([lo, hi], 0).astype(jnp.bfloat16)


def recur_kernel(
    n, x_hbm, y_hbm, gp_hbm, kvp_hbm, cw_ref, cb_ref, gs_ref, gb_ref, rate_ref, kvs_ref, rows_ref,
    mixed_hbm, kv_hbm,
    xv, yv, gpv, kvpv, xs, g, convb, pbuf, sbuf, gel, perm, unperm, halo, summ, gath, inc8,
    kvacc, kvrecv, kvbuf, mixv, masks_ref,
    load_sem, halo_sem, st_send, st_recv, kvx_sem, fwd_send, fwd_recv, pt_send, pt_recv, out_sem,
):
    me = lax.axis_index("tm")
    half = lax.axis_index("mp")
    T, C = xv.shape
    nb = C // HD
    steps = T // RUNS

    loads = [
        pltpu.make_async_copy(s, d, load_sem.at[i])
        for i, (s, d) in enumerate(((x_hbm, xv), (gp_hbm, gpv), (y_hbm, yv), (kvp_hbm, kvpv)))
    ]
    for c in loads:
        c.start()

    barrier = pltpu.get_barrier_semaphore()
    for k in range(1, n):
        pl.semaphore_signal(
            barrier, inc=1, device_id={"tm": lax.rem(me + k, n)}, device_id_type=MESH
        )
    pl.semaphore_signal(barrier, inc=1, device_id={"mp": 1 - half}, device_id_type=MESH)

    row = lax.broadcasted_iota(jnp.int32, (T, T), 0)
    col = lax.broadcasted_iota(jnp.int32, (T, T), 1)
    sh = steps.bit_length() - 1
    at_row = lax.bitwise_and(row, RUNS - 1) * steps + lax.shift_right_logical(row, 3)
    perm[...] = (at_row == col).astype(jnp.float32).astype(jnp.bfloat16)
    at_col = lax.bitwise_and(col, RUNS - 1) * steps + lax.shift_right_logical(col, 3)
    unperm[...] = (at_col == row).astype(jnp.float32).astype(jnp.bfloat16)
    masks_ref[...] = lax.dot_general(
        perm[...], rows_ref[...], (((1,), (1,)), ((), ())), preferred_element_type=jnp.float32
    )

    pl.semaphore_wait(barrier, n)
    halo_copy = pltpu.make_async_remote_copy(
        src_ref=x_hbm.at[pl.ds(T - 16, 16), :], dst_ref=halo,
        send_sem=halo_sem.at[0], recv_sem=halo_sem.at[1],
        device_id={"tm": lax.rem(me + 1, n)}, device_id_type=MESH,
    )

    @pl.when(me < n - 1)
    def _():
        halo_copy.start()

    @pl.when(me == 0)
    def _():
        halo[...] = jnp.zeros_like(halo)

    loads[0].wait()

    @pl.when(me > 0)
    def _():
        halo_copy.wait_recv()

    loads[1].wait()

    def block(b, _):
        cs = pl.ds(pl.multiple_of(b * HD, HD), HD)
        xp = jnp.dot(perm[...], xv[:, cs], preferred_element_type=jnp.float32)
        xs[pl.ds(24, T), :] = xp
        first = lax.broadcasted_iota(jnp.int32, (RUNS, HD), 0) == 0
        halo_f = halo[:, cs].astype(jnp.float32)
        for j in range(1, CONV):
            tail = xs[pl.ds(24 + T - 8 * j, 8), :]
            rolled = pltpu.roll(tail, 1, 0)
            xs[pl.ds(24 - 8 * j, 8), :] = jnp.where(first, halo_f[16 - j:17 - j], rolled)
        bias = cb_ref[:, cs]
        taps = [cw_ref[pl.ds(j, 1), cs] for j in range(CONV)]

        def conv_rows(i, _):
            r0 = pl.multiple_of(i * 64, 64)
            total = taps[0] * xs[pl.ds(r0 + 24, 64), :]
            for j in range(1, CONV):
                same = masks_ref[pl.ds(r0, 64), j - 1:j]
                total = total + taps[j] * (xs[pl.ds(r0 + 24 - 8 * j, 64), :] * same)
            convb[pl.ds(r0, 64), :] = (total + bias).astype(jnp.bfloat16)
            return 0

        lax.fori_loop(0, T // 64, conv_rows, 0, unroll=True)
        scales = gs_ref[b]
        gw = scaled(gpv[b], scales[0:1], scales[1:2])
        g[...] = jnp.dot(convb[...], gw, preferred_element_type=jnp.float32)
        b0, b1 = gb_ref[0:1, cs], gb_ref[1:2, cs]
        rate = -8.0 * rate_ref[:, cs]

        def rows(i, carry):
            prod, state = carry
            r0 = pl.multiple_of(i * 64, 64)
            rs = pl.ds(r0, 64)
            recur = sigmoid(g[rs, :HD] + b0)
            gate = sigmoid(g[rs, HD:] + b1)
            keep = masks_ref[rs, 0:1]
            e = expm1_small(recur * rate)
            a = (1.0 + e) * keep
            q = -e * (2.0 + e)
            m = q * lax.rsqrt(jnp.maximum(q, 1e-37))
            m = 1.0 + keep * (m - 1.0)
            u = gate * convb[rs, :].astype(jnp.float32) * m
            for k in range(8):
                ak = a[8 * k:8 * k + 8]
                prod = ak * prod
                state = ak * state + u[8 * k:8 * k + 8]
                pbuf[pl.ds(r0 + 8 * k, 8), cs] = prod
                sbuf[pl.ds(r0 + 8 * k, 8), cs] = state
            return prod, state

        lax.fori_loop(
            0, T // 64, rows, (jnp.ones((RUNS, HD), jnp.float32), jnp.zeros((RUNS, HD), jnp.float32)),
            unroll=2,
        )
        return 0

    lax.fori_loop(0, nb, block, 0)

    p_end = pbuf[pl.ds(T - 8, 8), :]
    s_end = sbuf[pl.ds(T - 8, 8), :]
    dp, ds = p_end[0:1], s_end[0:1]
    for s in range(1, RUNS):
        ds = p_end[s:s + 1] * ds + s_end[s:s + 1]
        dp = p_end[s:s + 1] * dp
    summ[0:1, :] = dp
    summ[1:2, :] = ds

    def state_copy(k):
        return pltpu.make_async_remote_copy(
            src_ref=summ, dst_ref=gath.at[k], send_sem=st_send.at[k], recv_sem=st_recv.at[k],
            device_id={"tm": lax.rem(me + k, n)}, device_id_type=MESH,
        )

    for k in range(1, n):
        @pl.when(me + k < n)
        def _(k=k):
            state_copy(k).start()

    loads[2].wait()

    def gelu_block(b, _):
        cs = pl.ds(pl.multiple_of(b * HD, HD), HD)
        gel[:, cs] = gelu(jnp.dot(perm[...], yv[:, cs], preferred_element_type=jnp.float32))
        return 0

    lax.fori_loop(0, nb, gelu_block, 0)
    loads[3].wait()

    inc8[0:1, :] = jnp.zeros((1, C), jnp.float32)
    for k in range(n - 1, 0, -1):
        @pl.when(me >= k)
        def _(k=k):
            state_copy(k).wait_recv()
            inc8[0:1, :] = gath[k, 0:1, :] * inc8[0:1, :] + gath[k, 1:2, :]
    cur = inc8[0:1, :]
    for s in range(RUNS - 1):
        cur = p_end[s:s + 1] * cur + s_end[s:s + 1]
        inc8[s + 1:s + 2, :] = cur

    kvacc[...] = jnp.zeros_like(kvacc)

    def mix_block(b, _):
        cs = pl.ds(pl.multiple_of(b * HD, HD), HD)
        entering = jnp.concatenate([inc8[:, cs]] * 8, 0)

        def mix_rows(i, _):
            rs = pl.ds(pl.multiple_of(i * 64, 64), 64)
            state = sbuf[rs, cs] + pbuf[rs, cs] * entering
            convb[rs, :] = (state * gel[rs, cs]).astype(jnp.bfloat16)
            return 0

        lax.fori_loop(0, T // 64, mix_rows, 0, unroll=True)
        mixed = jnp.dot(
            unperm[...], convb[...], preferred_element_type=jnp.float32
        ).astype(jnp.bfloat16)
        mixv[:, cs] = mixed
        kw = scaled(
            kvpv[pl.ds(pl.multiple_of(b * HD, HD), HD), :],
            kvs_ref[pl.ds(2 * b, 1), :], kvs_ref[pl.ds(2 * b + 1, 1), :],
        )
        kvacc[...] += jnp.dot(mixed, kw, preferred_element_type=jnp.float32)
        return 0

    lax.fori_loop(0, nb, mix_block, 0)
    mixed_out = pltpu.make_async_copy(mixv, mixed_hbm, out_sem.at[0])
    mixed_out.start()

    own_cols = pl.ds(pl.multiple_of(half * HD, HD), HD)
    their_cols = pl.ds(pl.multiple_of((1 - half) * HD, HD), HD)
    partner = {"mp": 1 - half}
    exchange = pltpu.make_async_remote_copy(
        src_ref=kvacc.at[:, their_cols], dst_ref=kvrecv,
        send_sem=kvx_sem.at[0], recv_sem=kvx_sem.at[1], device_id=partner, device_id_type=MESH,
    )
    exchange.start()
    exchange.wait_recv()
    kvbuf[0, half] = (kvacc[:, own_cols] + kvrecv[...]).astype(jnp.bfloat16)

    odd = lax.rem(me, 2) == 1
    even = lax.rem(me, 2) == 0

    part = T // 2

    def forward(src, dst, sem, to, ch):
        rs = pl.ds(ch * part, part)
        return pltpu.make_async_remote_copy(
            src_ref=kvbuf.at[src, half, rs, :], dst_ref=kvbuf.at[dst, half, rs, :],
            send_sem=fwd_send.at[2 * sem + ch], recv_sem=fwd_recv.at[2 * dst + ch],
            device_id={"tm": lax.rem(me + to + n, n)}, device_id_type=MESH,
        )

    def share(slot, ch):
        rs = pl.ds(ch * part, part)
        return pltpu.make_async_remote_copy(
            src_ref=kvbuf.at[slot, half, rs, :], dst_ref=kvbuf.at[slot, half, rs, :],
            send_sem=pt_send.at[2 * slot + ch], recv_sem=pt_recv.at[2 * slot + ch],
            device_id=partner, device_id_type=MESH,
        )

    def arrived(slot, ch):
        forward(0, slot, 0, 2, ch).wait_recv()

    z_first = [forward(0, 2, 0, 2, ch) for ch in range(2)]
    z_second = [forward(2, 4, 1, 2, ch) for ch in range(2)]
    even_a = [forward(0, 1, 2, 1, ch) for ch in range(2)]
    even_b = [forward(2, 3, 3, 1, ch) for ch in range(2)]
    odd_a = [forward(2, 1, 2, -1, ch) for ch in range(2)]
    odd_b = [forward(4, 3, 3, -1, ch) for ch in range(2)]
    ahead = me + 2 < n

    def when(cond, do):
        pl.when(cond)(do)

    for ch in range(2):
        when(ahead, z_first[ch].start)
        when(even, even_a[ch].start)
    for ch in range(2):
        share(0, ch).start()

    for ch in range(2):
        @pl.when(me >= 2)
        def _(ch=ch):
            arrived(2, ch)
            when(ahead, z_second[ch].start)
            when(even, even_b[ch].start)
            when(odd, odd_a[ch].start)
            share(2, ch).start()

    for slot in (1, 4, 3):
        for ch in range(2):
            @pl.when(me >= slot)
            def _(ch=ch, slot=slot):
                arrived(slot, ch)
                if slot == 4:
                    when(odd, odd_b[ch].start)
                share(slot, ch).start()

    outs = [pltpu.make_async_copy(kvbuf.at[k], kv_hbm.at[4 - k], out_sem.at[1 + k]) for k in range(5)]
    for k in range(5):
        @pl.when(me >= k)
        def _(k=k):
            share(k, 0).wait()
            share(k, 1).wait()
            outs[k].start()

    for k in range(1, n):
        @pl.when(me + k < n)
        def _(k=k):
            state_copy(k).wait_send()

    @pl.when(me < n - 1)
    def _():
        halo_copy.wait_send()

    exchange.wait_send()
    for ch in range(2):
        when(ahead, z_first[ch].wait_send)
        when(even, even_a[ch].wait_send)

        @pl.when(me >= 2)
        def _(ch=ch):
            when(ahead, z_second[ch].wait_send)
            when(even, even_b[ch].wait_send)
            when(odd, odd_a[ch].wait_send)

        when(odd & (me >= 4), odd_b[ch].wait_send)
    for k in range(5):
        when(me >= k, outs[k].wait)
    mixed_out.wait()


def attend_kernel(lo_ref, q_ref, kv_ref, kid_ref, mixed_in, o_ref, mixed_out, bias, scores, acc, top, low):
    j = pl.program_id(0)
    heads = q_ref.shape[1] // HD
    mixed_out[...] = mixed_in[...]
    lo = lo_ref[j]
    hi = WINDOW // TILE + j + 1
    per = kv_ref.shape[2] // TILE
    c = HD ** (-0.5) * 1.4426950408889634
    offset = lax.broadcasted_iota(jnp.int32, (TILE, TILE), 0) - lax.broadcasted_iota(
        jnp.int32, (TILE, TILE), 1
    )
    own = jnp.where(offset == 0, kid_ref[WINDOW // TILE + j], 0.0)
    qid = jnp.sum(own, axis=1, keepdims=True)
    top[...] = jnp.full_like(top, -3e38)
    low[...] = jnp.zeros_like(low)
    acc[...] = jnp.zeros_like(acc)

    def score(t, _):
        blk, r = t // per, lax.rem(t, per)
        keys = kv_ref[blk, 0, pl.ds(pl.multiple_of(r * TILE, TILE), TILE), :]
        back = offset + (WINDOW + (j - t) * TILE)
        ok = (back >= 0) & (back < WINDOW) & (kid_ref[t] == qid)
        bias[...] = jnp.where(ok, 0.0, -1e30)
        for h in range(heads):
            s = lax.dot_general(
                q_ref[:, h * HD:(h + 1) * HD], keys, (((1,), (1,)), ((), ())),
                preferred_element_type=jnp.float32,
            ) + bias[...]
            scores[h, t] = s
            top[h] = jnp.maximum(top[h], jnp.maximum(s[:, :128], s[:, 128:]))
        return 0

    lax.fori_loop(lo, hi, score, 0)
    for h in range(heads):
        top[h] = jnp.broadcast_to(jnp.max(top[h], axis=1, keepdims=True), (TILE, 128))

    def weigh(t, _):
        blk, r = t // per, lax.rem(t, per)
        values = kv_ref[blk, 1, pl.ds(pl.multiple_of(r * TILE, TILE), TILE), :]
        for h in range(heads):
            m = top[h]
            s = scores[h, t]
            w = [jnp.exp2((s[:, i * 128:(i + 1) * 128] - m) * c) for i in range(2)]
            low[h] += w[0] + w[1]
            acc[h] += jnp.dot(
                jnp.concatenate(w, 1).astype(jnp.bfloat16), values, preferred_element_type=jnp.float32
            )
        return 0

    lax.fori_loop(lo, hi, weigh, 0)
    for h in range(heads):
        total = jnp.sum(low[h], axis=1, keepdims=True)
        o_ref[:, h * HD:(h + 1) * HD] = (acc[h] * (1.0 / total)).astype(jnp.bfloat16)


def local(
    n, branch_x, branch_y, queries, conv_weight, conv_bias, gate_panel, gate_scale, gate_bias,
    decay_rate, kv_panel, kv_scale, segment_ids,
):
    T, C = branch_x.shape
    f32, bf16 = jnp.float32, jnp.bfloat16
    heads = queries.shape[1] // HD
    first_row = lax.axis_index("tm") * T
    padded_ids = jnp.concatenate([-jnp.ones((WINDOW,), jnp.int32), segment_ids])
    key_ids = lax.dynamic_slice_in_dim(padded_ids, first_row, WINDOW + T)
    own_ids = key_ids[WINDOW:]
    masks = jnp.stack(
        [(key_ids[WINDOW - j:WINDOW - j + T] == own_ids).astype(bf16) for j in range(1, CONV)]
        + [jnp.zeros((T,), bf16)] * (128 - CONV + 1)
    )
    vmem, anyw = pl.BlockSpec(memory_space=pltpu.VMEM), pl.BlockSpec(memory_space=pl.ANY)
    dma = pltpu.SemaphoreType.DMA
    mixed, kv = pl.pallas_call(
        functools.partial(recur_kernel, n),
        out_shape=(
            jax.ShapeDtypeStruct((T, C), bf16), jax.ShapeDtypeStruct((5, 2, T, HD), bf16),
        ),
        in_specs=[anyw] * 4 + [vmem] * 7,
        out_specs=(anyw, anyw),
        scratch_shapes=[
            pltpu.VMEM((T, C), bf16), pltpu.VMEM((T, C), bf16),
            pltpu.VMEM(gate_panel.shape, bf16), pltpu.VMEM(kv_panel.shape, bf16),
            pltpu.VMEM((T + 24, HD), f32), pltpu.VMEM((T, 2 * HD), f32), pltpu.VMEM((T, HD), bf16),
            pltpu.VMEM((T, C), f32), pltpu.VMEM((T, C), f32), pltpu.VMEM((T, C), f32),
            pltpu.VMEM((T, T), bf16), pltpu.VMEM((T, T), bf16), pltpu.VMEM((16, C), bf16),
            pltpu.VMEM((2, C), f32), pltpu.VMEM((n, 2, C), f32), pltpu.VMEM((RUNS, C), f32),
            pltpu.VMEM((T, 2 * HD), f32), pltpu.VMEM((T, HD), f32),
            pltpu.VMEM((5, 2, T, HD), bf16), pltpu.VMEM((T, C), bf16),
            pltpu.VMEM((T, 128), f32),
            dma((4,)), dma((2,)), dma((n,)), dma((n,)), dma((2,)), dma((8,)), dma((10,)),
            dma((10,)), dma((10,)), dma((6,)),
        ],
        compiler_params=pltpu.CompilerParams(
            collective_id=0, has_side_effects=True, vmem_limit_bytes=56 * 1024 * 1024
        ),
        name="recurrence",
    )(
        branch_x, branch_y, gate_panel, kv_panel, conv_weight, conv_bias[None], gate_scale,
        gate_bias, decay_rate[None], kv_scale, masks,
    )
    tiles = (WINDOW + T) // TILE
    row0 = jnp.arange(T // TILE, dtype=jnp.int32) * TILE
    doc = jnp.sum((key_ids[None, :] < own_ids[::TILE][:, None]).astype(jnp.int32), 1)
    lo = jnp.maximum(doc, row0 + 1) // TILE
    attended, mixed = pl.pallas_call(
        attend_kernel,
        out_shape=(
            jax.ShapeDtypeStruct(queries.shape, bf16), jax.ShapeDtypeStruct((T, C), bf16),
        ),
        grid_spec=pltpu.PrefetchScalarGridSpec(
            num_scalar_prefetch=1,
            grid=(T // TILE,),
            in_specs=[
                pl.BlockSpec((TILE, heads * HD), lambda j, lo: (j, 0)),
                pl.BlockSpec(memory_space=pltpu.VMEM),
                pl.BlockSpec(memory_space=pltpu.VMEM),
                pl.BlockSpec((TILE, C), lambda j, lo: (j, 0)),
            ],
            out_specs=(
                pl.BlockSpec((TILE, heads * HD), lambda j, lo: (j, 0)),
                pl.BlockSpec((TILE, C), lambda j, lo: (j, 0)),
            ),
            scratch_shapes=[
                pltpu.VMEM((TILE, TILE), f32), pltpu.VMEM((heads, tiles, TILE, TILE), f32),
                pltpu.VMEM((heads, TILE, HD), f32), pltpu.VMEM((heads, TILE, 128), f32),
                pltpu.VMEM((heads, TILE, 128), f32),
            ],
        ),
        compiler_params=pltpu.CompilerParams(vmem_limit_bytes=56 * 1024 * 1024),
        name="attention",
    )(lo, queries, kv, key_ids.astype(f32).reshape(tiles, 1, TILE), mixed)
    return (mixed, attended)


def solution(mesh):
    rows = P(("groups", "tm"), "mp")
    in_specs = (
        rows, rows, rows, P(None, "mp"), P("mp"), P("mp", None, None), P("mp", None, None),
        P(None, "mp"), P("mp"), P("mp", None), P("mp", None), P("groups"),
    )
    return jax.shard_map(
        functools.partial(local, mesh.shape["tm"]), mesh=mesh, in_specs=in_specs,
        out_specs=(rows, rows), check_vma=False,
    )
```
